32 devices in a mesh: dp: 4 (over y, x), row: 8 (over z, core).
Axes of the slice: x: 2, y: 2, z: 4, core: 2. Of those that a mesh axis runs over, the one named last changes fastest.
Arguments:
- stacked_sequences: bfloat16 [4, 32, 256, 768], P('dp', 'row'), may hold values from -8 to 8
- upstream_derivative: bfloat16 [4, 32, 256, 768], P('dp', 'row'), may hold values from -6 to 6
- asking_projection_weights: bfloat16 [768, 768], replicated, may hold values from -1 to 1
- lookup_projection_weights: bfloat16 [768, 768], replicated, may hold values from -1 to 1
- content_projection_weights: bfloat16 [768, 768], replicated, may hold values from -0.21875 to 0.21875
- final_projection_weights: bfloat16 [768, 768], replicated, may hold values from -0.21875 to 0.21875
Outputs:
- input_derivative: bfloat16 [4, 32, 256, 768], P('dp', 'row')
- d_query: float32 [768, 768], P(('dp', 'row'))
- d_key: float32 [768, 768], P(('dp', 'row'))
- d_value: float32 [768, 768], P(('dp', 'row'))
- d_outw: float32 [768, 768], P(('dp', 'row'))
The draws below stay inside these ranges and needn't reach their ends.
All inputs are finite; a program needn't handle non-finite values.
Results may differ from the reference program's by a relative error of at most 0.015.
Values may be sent and summed in bfloat16 or wider, within the bound.
A program may use at most 128 MiB of HBM per device.

```python
import math
import jax
import jax.numpy as jnp
from jax import lax

D = 768
H = 12
C = 256
ROWS = 32
ALN = 4


def draw_stacked_sequences(key, part):
    key = jax.random.fold_in(key, 7)
    first = jax.random.fold_in(key, 0)
    return jnp.clip(jax.random.normal(first, (ALN, ROWS, C, D), jnp.float32), -6.0, 6.0).astype(jnp.bfloat16)


def draw_asking_projection_weights(key, part):
    key = jax.random.fold_in(key, 11)
    return (jnp.clip(jax.random.normal(key, (D, D), jnp.float32), -5.0, 5.0) / math.sqrt(D)).astype(jnp.bfloat16)


def draw_lookup_projection_weights(key, part):
    key = jax.random.fold_in(key, 12)
    fresh = jnp.clip(jax.random.normal(key, (D, D), jnp.float32), -5.0, 5.0) / math.sqrt(D)
    return fresh.astype(jnp.bfloat16)


def shard_levels(key, dims, cuts, smallest, top_value):
    level, own = 1.0, jax.random.fold_in(key, 6)
    for position, blocks in cuts:
        heights = jnp.exp(jax.random.uniform(jax.random.fold_in(own, position), (blocks,), jnp.float32, smallest / len(cuts), top_value / len(cuts)))
        level = level * jnp.repeat(heights, dims[position] // blocks).reshape([-1 if axis == position else 1 for axis in range(len(dims))])
    return level


def scatter_about(own_key, shape, spread, bound, cuts=(), held_as=jnp.bfloat16):
    level = shard_levels(own_key, shape, cuts, -0.22, 0.18) if cuts else 1.0
    entries = jax.random.normal(own_key, shape, jnp.float32) * spread * level
    return jnp.minimum(jnp.maximum(entries, -bound), bound).astype(held_as)


def setup_inputs(seed: int = 0) -> dict:
    splits = jax.random.split(jax.random.key(seed), 7)
    stacked_sequences = draw_stacked_sequences(jax.random.fold_in(splits[6], 71), 0)
    upstream_derivative = scatter_about(splits[1], (ALN, ROWS, C, D), 1.0, 6.0, ((0, 4), (1, 8)))
    asking_projection_weights = draw_asking_projection_weights(jax.random.fold_in(splits[6], 71), 0)
    lookup_projection_weights = draw_lookup_projection_weights(jax.random.fold_in(splits[6], 71), 0)
    content_projection_weights = scatter_about(splits[4], (D, D), D ** -0.5, 0.21875)
    final_projection_weights = scatter_about(splits[5], (D, D), D ** -0.5, 0.21875)
    return {"stacked_sequences": stacked_sequences, "upstream_derivative": upstream_derivative, "asking_projection_weights": asking_projection_weights, "lookup_projection_weights": lookup_projection_weights, "content_projection_weights": content_projection_weights, "final_projection_weights": final_projection_weights}


def outer(left, right):
    return lax.dot_general(left, right, (((0,), (0,)), ((), ())), preferred_element_type=jnp.float32)

def reference(stacked_sequences, upstream_derivative, asking_projection_weights, lookup_projection_weights, content_projection_weights, final_projection_weights):
    depth = D // H
    scale = 1.0 / (math.sqrt(depth) * math.sqrt(ROWS))

    def lone_element(carry, pair):
        xa, ga = pair
        merged_sequence_sites = xa.reshape(-1, D)
        gflat = ga.reshape(-1, D)

        def project(weight):
            return jnp.dot(merged_sequence_sites, weight, preferred_element_type=jnp.float32).astype(jnp.bfloat16)
        query = project(asking_projection_weights)
        keys = project(lookup_projection_weights)
        values = project(content_projection_weights)
        d_out = jnp.dot(gflat, final_projection_weights.T, preferred_element_type=jnp.float32).astype(jnp.bfloat16)
        shaped = (ROWS, C, H, depth)
        qf = query.reshape(shaped).astype(jnp.float32)
        kf = keys.reshape(shaped).astype(jnp.float32)
        vf = values.reshape(shaped).astype(jnp.float32)
        of = d_out.reshape(shaped).astype(jnp.float32)
        logits = jnp.einsum('rihe,rjhe->hij', qf, kf) * scale
        probs = jax.nn.softmax(logits, axis=-1)
        probs_b = probs.astype(jnp.bfloat16)
        pf = probs_b.astype(jnp.float32)
        attended = jnp.einsum('hij,rjhe->rihe', pf, vf).astype(jnp.bfloat16)
        dprobs = jnp.einsum('rihe,rjhe->hij', of, vf)
        inner = lax.optimization_barrier(jnp.sum(probs * dprobs, axis=-1, keepdims=True))
        dscores = (probs * (dprobs - inner) * scale).astype(jnp.bfloat16).astype(jnp.float32)
        dq = jnp.einsum('hij,rjhe->rihe', dscores, kf).astype(jnp.bfloat16).reshape(-1, D)
        dk = jnp.einsum('hij,rihe->rjhe', dscores, qf).astype(jnp.bfloat16).reshape(-1, D)
        dv = jnp.einsum('hij,rihe->rjhe', pf, of).astype(jnp.bfloat16).reshape(-1, D)
        d_x = (jnp.dot(dq, asking_projection_weights.T, preferred_element_type=jnp.float32) + jnp.dot(dk, lookup_projection_weights.T, preferred_element_type=jnp.float32) + jnp.dot(dv, content_projection_weights.T, preferred_element_type=jnp.float32)).astype(jnp.bfloat16)
        grads = (outer(merged_sequence_sites, dq), outer(merged_sequence_sites, dk), outer(merged_sequence_sites, dv), outer(attended.reshape(-1, D), gflat))
        carry = tuple((a + b for a, b in zip(carry, grads)))
        return (carry, d_x.reshape(ROWS, C, D))
    beginning_position = tuple((jnp.zeros((D, D), jnp.float32) for index in range(4)))
    cumulative_partial_sums_list, input_derivative = lax.scan(lone_element, beginning_position, (stacked_sequences, upstream_derivative))
    return (input_derivative, cumulative_partial_sums_list[0], cumulative_partial_sums_list[1], cumulative_partial_sums_list[2], cumulative_partial_sums_list[3])
```

```python
import math

import jax
import jax.numpy as jnp
from jax import lax
from jax.sharding import PartitionSpec as P

H = 12


def outer(left, right):
    return lax.dot_general(
        left, right, (((0,), (0,)), ((), ())), preferred_element_type=jnp.float32
    )


def score_grads(probs, dprobs, scale):
    inner = jnp.sum(probs * dprobs, axis=-1, keepdims=True)
    return (probs * (dprobs - inner) * scale).astype(jnp.bfloat16)


def body(
    stacked_sequences,
    upstream_derivative,
    asking_projection_weights,
    lookup_projection_weights,
    content_projection_weights,
    final_projection_weights,
):
    sequences_each_processor = stacked_sequences.shape[1]
    number_of_sites = stacked_sequences.shape[2]
    embedding_dimension = stacked_sequences.shape[3]
    depth = embedding_dimension // H
    total_rows = sequences_each_processor * lax.axis_size("row")
    scale = 1.0 / (math.sqrt(depth) * math.sqrt(total_rows))
    merged_sequence_sites = stacked_sequences.reshape(-1, embedding_dimension)
    gflat = upstream_derivative.reshape(-1, embedding_dimension)
    shaped = (sequences_each_processor, number_of_sites, H, depth)

    def project(weight):
        return jnp.dot(merged_sequence_sites, weight, preferred_element_type=jnp.float32).astype(
            jnp.bfloat16
        )

    query = project(asking_projection_weights).reshape(shaped)
    keys = project(lookup_projection_weights).reshape(shaped)
    values = project(content_projection_weights).reshape(shaped)
    d_out = (
        jnp.dot(gflat, final_projection_weights.T, preferred_element_type=jnp.float32)
        .astype(jnp.bfloat16)
        .reshape(shaped)
    )
    part_logits = jnp.einsum("rihe,rjhe->hij", query, keys, preferred_element_type=jnp.float32)
    part_dprob = jnp.einsum("rihe,rjhe->hij", d_out, values, preferred_element_type=jnp.float32)
    lines = (H * number_of_sites, number_of_sites)
    logits = (
        lax.psum_scatter(part_logits.reshape(lines), "row", scatter_dimension=0, tiled=True) * scale
    )
    dprobs = lax.psum_scatter(part_dprob.reshape(lines), "row", scatter_dimension=0, tiled=True)
    probs = jax.nn.softmax(logits, axis=-1)
    my_dscores = score_grads(probs, dprobs, scale)
    whole = (H, number_of_sites, number_of_sites)
    probs_b = lax.all_gather(probs.astype(jnp.bfloat16), "row", axis=0, tiled=True).reshape(whole)
    dscores = lax.all_gather(my_dscores, "row", axis=0, tiled=True).reshape(whole)
    attended = jnp.einsum(
        "hij,rjhe->rihe", probs_b, values, preferred_element_type=jnp.float32
    ).astype(jnp.bfloat16)
    d_q = (
        jnp.einsum("hij,rjhe->rihe", dscores, keys, preferred_element_type=jnp.float32)
        .astype(jnp.bfloat16)
        .reshape(-1, embedding_dimension)
    )
    d_k = (
        jnp.einsum("hij,rihe->rjhe", dscores, query, preferred_element_type=jnp.float32)
        .astype(jnp.bfloat16)
        .reshape(-1, embedding_dimension)
    )
    d_v = (
        jnp.einsum("hij,rihe->rjhe", probs_b, d_out, preferred_element_type=jnp.float32)
        .astype(jnp.bfloat16)
        .reshape(-1, embedding_dimension)
    )
    d_input = (
        (
            jnp.dot(d_q, asking_projection_weights.T, preferred_element_type=jnp.float32)
            + jnp.dot(d_k, lookup_projection_weights.T, preferred_element_type=jnp.float32)
            + jnp.dot(d_v, content_projection_weights.T, preferred_element_type=jnp.float32)
        )
        .astype(jnp.bfloat16)
        .reshape(stacked_sequences.shape)
    )
    grads = (
        outer(merged_sequence_sites, d_q),
        outer(merged_sequence_sites, d_k),
        outer(merged_sequence_sites, d_v),
        outer(attended.reshape(-1, embedding_dimension), gflat),
    )
    partial_sums = (
        lax.psum_scatter(
            grads[0].astype(jnp.bfloat16), "dp", scatter_dimension=0, tiled=True
        ).astype(jnp.float32),
        lax.psum_scatter(
            grads[1].astype(jnp.bfloat16), "dp", scatter_dimension=0, tiled=True
        ).astype(jnp.float32),
        lax.psum_scatter(
            grads[2].astype(jnp.bfloat16), "dp", scatter_dimension=0, tiled=True
        ).astype(jnp.float32),
        lax.psum_scatter(
            grads[3].astype(jnp.bfloat16), "dp", scatter_dimension=0, tiled=True
        ).astype(jnp.float32),
    )
    reduced = (
        lax.psum_scatter(
            partial_sums[0].astype(jnp.bfloat16), "row", scatter_dimension=0, tiled=True
        ).astype(jnp.float32),
        lax.psum_scatter(
            partial_sums[1].astype(jnp.bfloat16), "row", scatter_dimension=0, tiled=True
        ).astype(jnp.float32),
        lax.psum_scatter(
            partial_sums[2].astype(jnp.bfloat16), "row", scatter_dimension=0, tiled=True
        ).astype(jnp.float32),
        lax.psum_scatter(
            partial_sums[3].astype(jnp.bfloat16), "row", scatter_dimension=0, tiled=True
        ).astype(jnp.float32),
    )
    return (d_input, reduced[0], reduced[1], reduced[2], reduced[3])


def solution(mesh):
    return jax.shard_map(
        body,
        mesh=mesh,
        in_specs=(P("dp", "row", None, None), P("dp", "row", None, None), P(), P(), P(), P()),
        out_specs=(
            P("dp", "row", None, None),
            P(("dp", "row"), None),
            P(("dp", "row"), None),
            P(("dp", "row"), None),
            P(("dp", "row"), None),
        ),
        check_vma=False,
    )
```

```python
import functools
import math

import jax
import jax.numpy as jnp
from jax import lax
from jax.experimental import pallas as pl
from jax.experimental.pallas import tpu as pltpu
from jax.sharding import PartitionSpec as P

H = 12
BF = jnp.bfloat16
F32 = jnp.float32
NT = (((1,), (1,)), ((), ()))
TN = (((0,), (0,)), ((), ()))
NN = (((1,), (0,)), ((), ()))


def dot(a, b, dims=NN):
    return lax.dot_general(a, b, dims, preferred_element_type=F32)


def kernel(
    nb, seqs, sites, scale,
    x, g, wq, wk, wv, wo,
    dx, grads,
    q, k, v, do, att, dq, dk, dv, acc_s, acc_d, probs, dsc, out_d, in0_s, in0_d, *rest,
):
    in_s = (in0_s,) + rest[: nb - 1]
    in_d = (in0_d,) + rest[nb - 1 : 2 * nb - 2]
    rs_send, rs_recv, ag_send, ag_recv = rest[2 * nb - 2 :]
    width = x.shape[1]
    pairs = width // 128
    lines = 2 * sites
    me = lax.axis_index("row")
    bits = [lax.rem(me // (1 << b), 2) for b in range(nb)]
    peers = [me + (1 - 2 * bits[b]) * (1 << b) for b in range(nb)]
    offs = [0]
    for b in range(nb):
        offs.append(pl.multiple_of(offs[b] + bits[b] * (lines >> (b + 1)), lines >> (b + 1)))

    barrier = pltpu.get_barrier_semaphore()
    for peer in peers:
        pl.semaphore_signal(
            barrier, inc=1, device_id={"row": peer}, device_id_type=pl.DeviceIdType.MESH
        )
    pl.semaphore_wait(barrier, nb)

    def remote(src, dst, send, recv, peer):
        return pltpu.make_async_remote_copy(
            src_ref=src, dst_ref=dst, send_sem=send, recv_sem=recv,
            device_id={"row": peer}, device_id_type=pl.DeviceIdType.MESH,
        )

    def scatter_copies(b, c):
        half = lines >> (b + 1)
        gone = pl.multiple_of(offs[b] + (1 - bits[b]) * half, half)
        d_src = acc_d if b == 0 else out_d
        return (
            remote(acc_s.at[c, pl.ds(gone, half)], in_s[b].at[c],
                   rs_send.at[0, b, c], rs_recv.at[0, b, c], peers[b]),
            remote(d_src.at[c, pl.ds(gone, half)], in_d[b].at[c],
                   rs_send.at[1, b, c], rs_recv.at[1, b, c], peers[b]),
        )

    def gather_copies(b, c):
        half = lines >> (b + 1)
        mine = pl.ds(offs[b + 1], half)
        return tuple(
            remote(ref.at[c, mine], ref.at[c, mine],
                   ag_send.at[n, b, c], ag_recv.at[n, b, c], peers[b])
            for n, ref in enumerate((probs, dsc))
        )

    low = lax.broadcasted_iota(jnp.int32, (sites, 128), 1) < 64

    def parts(ref, c):
        cols = pl.ds(pl.multiple_of(c * 128, 128), 128)
        return [ref[r * sites : (r + 1) * sites, cols] for r in range(seqs)]

    def head_of(blocks, first):
        zero = jnp.zeros((sites, 128), BF)
        return [jnp.where(low, t, zero) if first else jnp.where(low, zero, t) for t in blocks]

    def shares(c):
        @pl.when(lax.rem(c, 2) == 0)
        def _():
            cols = pl.ds(pl.multiple_of(c * 128, 128), 256)
            q[:, cols] = dot(x[...], wq[:, cols]).astype(BF)
            k[:, cols] = dot(x[...], wk[:, cols]).astype(BF)
            v[:, cols] = dot(x[...], wv[:, cols]).astype(BF)
            do[:, cols] = dot(g[...], wo[cols, :], NT).astype(BF)

        for left, right, acc in ((q, k, acc_s), (do, v, acc_d)):
            a = jnp.concatenate(parts(left, c), axis=1)
            blocks = parts(right, c)
            for n in range(2):
                acc[c, n * sites : (n + 1) * sites, :] = dot(
                    a, jnp.concatenate(head_of(blocks, n == 0), axis=1), NT
                )
        for copy in scatter_copies(0, c):
            copy.start()

    def join(b, c):
        half = lines >> (b + 1)
        for copy in scatter_copies(b, c):
            copy.wait()
        mine = pl.ds(offs[b + 1], half)
        acc_s[c, mine, :] = acc_s[c, mine, :] + in_s[b][c]
        acc_d[c, mine, :] = acc_d[c, mine, :] + in_d[b][c].astype(F32)
        if b + 1 < nb:
            quarter = half // 2
            gone = pl.ds(
                pl.multiple_of(offs[b + 1] + (1 - bits[b + 1]) * quarter, quarter), quarter
            )
            out_d[c, gone, :] = acc_d[c, gone, :].astype(BF)
            for copy in scatter_copies(b + 1, c):
                copy.start()
        else:
            logits = acc_s[c, mine, :] * scale
            e = jnp.exp(logits - jnp.max(logits, axis=-1, keepdims=True))
            p = e / jnp.sum(e, axis=-1, keepdims=True)
            d = acc_d[c, mine, :]
            inner = jnp.sum(p * d, axis=-1, keepdims=True)
            probs[c, mine, :] = p.astype(BF)
            dsc[c, mine, :] = (p * (d - inner) * scale).astype(BF)
            for copy in gather_copies(b, c):
                copy.start()

    def spread(b, c):
        for copy in gather_copies(b, c):
            copy.wait()
        if b > 0:
            for copy in gather_copies(b - 1, c):
                copy.start()
        else:
            use(c)

    def use(c):
        cols = pl.ds(pl.multiple_of(c * 128, 128), 128)

        def stacked(ref):
            blocks = parts(ref, c)
            return jnp.concatenate(
                [jnp.concatenate(head_of(blocks, n == 0), axis=1) for n in range(2)], axis=0
            )

        def put(ref, value):
            for r in range(seqs):
                ref[r * sites : (r + 1) * sites, cols] = value[:, r * 128 : (r + 1) * 128].astype(BF)

        p = probs[c]
        d = dsc[c]
        p_wide = jnp.concatenate([p[:sites], p[sites:]], axis=1)
        d_wide = jnp.concatenate([d[:sites], d[sites:]], axis=1)
        put(att, dot(p_wide, stacked(v)))
        put(dv, dot(p, stacked(do), TN))
        put(dq, dot(d_wide, stacked(k)))
        put(dk, dot(d, stacked(q), TN))

    def tick(t, carry):
        for stage in range(2 * nb, -1, -1):
            c = t - stage

            @pl.when(jnp.logical_and(c >= 0, c < pairs))
            def _(stage=stage, c=c):
                if stage == 0:
                    shares(c)
                elif stage <= nb:
                    join(stage - 1, c)
                else:
                    spread(2 * nb - stage, c)
        return carry

    lax.fori_loop(0, pairs + 2 * nb, tick, 0)

    def weights_block(n, carry):
        base = pl.multiple_of(n * 256, 256)
        cols = pl.ds(base, 256)
        grads[:, cols] = dot(x[...], dq[:, cols], TN).astype(BF)
        grads[:, pl.ds(base + width, 256)] = dot(x[...], dk[:, cols], TN).astype(BF)
        grads[:, pl.ds(base + 2 * width, 256)] = dot(x[...], dv[:, cols], TN).astype(BF)
        grads[:, pl.ds(base + 3 * width, 256)] = dot(att[...], g[:, cols], TN).astype(BF)
        return carry

    lax.fori_loop(0, width // 256, weights_block, 0)

    def rows_block(n, carry):
        rows = pl.ds(pl.multiple_of(n * 256, 256), 256)
        dx[rows, :] = (
            dot(dq[rows, :], wq[...], NT)
            + dot(dk[rows, :], wk[...], NT)
            + dot(dv[rows, :], wv[...], NT)
        ).astype(BF)
        return carry

    lax.fori_loop(0, x.shape[0] // 256, rows_block, 0)


def body(xs, gs, wq, wk, wv, wo):
    seqs, sites, width = xs.shape[1:]
    group = lax.axis_size("row")
    nb = group.bit_length() - 1
    pairs = width // 128
    lines = 2 * sites
    n = seqs * sites
    scale = 1.0 / (math.sqrt(width // H) * math.sqrt(seqs * group))
    vmem = pl.BlockSpec(memory_space=pltpu.VMEM)
    halves = [lines >> (b + 1) for b in range(nb)]
    act = pltpu.VMEM((n, width), BF)
    scratch = [act] * 8
    scratch += [pltpu.VMEM((pairs, lines, sites), F32)] * 2
    scratch += [pltpu.VMEM((pairs, lines, sites), BF)] * 3
    scratch += [pltpu.VMEM((pairs, halves[0], sites), F32)] * 2
    scratch += [pltpu.VMEM((pairs, h, sites), F32) for h in halves[1:]]
    scratch += [pltpu.VMEM((pairs, h, sites), BF) for h in halves[1:]]
    scratch += [pltpu.SemaphoreType.DMA((2, nb, pairs))] * 4
    dx, grads = pl.pallas_call(
        functools.partial(kernel, nb, seqs, sites, scale),
        out_shape=(
            jax.ShapeDtypeStruct((n, width), BF),
            jax.ShapeDtypeStruct((width, 4 * width), BF),
        ),
        in_specs=[vmem] * 6,
        out_specs=(vmem, vmem),
        scratch_shapes=scratch,
        compiler_params=pltpu.CompilerParams(
            collective_id=0, has_side_effects=True, vmem_limit_bytes=60 * 1024 * 1024
        ),
    )(xs.reshape(n, width), gs.reshape(n, width), wq, wk, wv, wo)
    part = lax.psum_scatter(grads, "dp", scatter_dimension=0, tiled=True)
    part = lax.psum_scatter(part, "row", scatter_dimension=0, tiled=True).astype(F32)
    return (dx.reshape(xs.shape),) + tuple(part[:, i * width : (i + 1) * width] for i in range(4))


def solution(mesh):
    return jax.shard_map(
        body,
        mesh=mesh,
        in_specs=(P("dp", "row", None, None), P("dp", "row", None, None), P(), P(), P(), P()),
        out_specs=(P("dp", "row", None, None),) + (P(("dp", "row"), None),) * 4,
        check_vma=False,
    )
```

```python
import functools
import math

import jax
import jax.numpy as jnp
from jax import lax
from jax.experimental import pallas as pl
from jax.experimental.pallas import tpu as pltpu
from jax.sharding import PartitionSpec as P

H = 12
BF = jnp.bfloat16
F32 = jnp.float32
NT = (((1,), (1,)), ((), ()))
TN = (((0,), (0,)), ((), ()))
NN = (((1,), (0,)), ((), ()))


def dot(a, b, dims=NN):
    return lax.dot_general(a, b, dims, preferred_element_type=F32)


def kernel(
    nb, group, copies, seqs, sites, scale,
    x, g, wq, wk, wv, wo,
    dx, grads,
    q, k, v, do, att, dq, dk, dv, acc_s, acc_d, probs, dsc, out_d, in0_s, in0_d, *rest,
):
    in_s = (in0_s,) + rest[: nb - 1]
    in_d = (in0_d,) + rest[nb - 1 : 2 * nb - 2]
    rs_send, rs_recv, ag_send, ag_recv = rest[2 * nb - 2 : 2 * nb + 2]
    width = x.shape[1]
    fold = grads.ndim == 3
    nd = copies.bit_length() - 1
    steps = nb + nd if fold else 0
    if fold:
        w_send, w_recv, held = rest[2 * nb + 2 : 2 * nb + 5]
        w_in = rest[2 * nb + 5 :]
    pairs = width // 128
    lines = 2 * sites
    me = lax.axis_index("row")
    bits = [lax.rem(me // (1 << b), 2) for b in range(nb)]
    peers = [me + (1 - 2 * bits[b]) * (1 << b) for b in range(nb)]
    offs = [0]
    for b in range(nb):
        offs.append(pl.multiple_of(offs[b] + bits[b] * (lines >> (b + 1)), lines >> (b + 1)))

    barrier = pltpu.get_barrier_semaphore()
    for peer in peers:
        pl.semaphore_signal(
            barrier, inc=1, device_id={"row": peer}, device_id_type=pl.DeviceIdType.MESH
        )
    if fold:
        mine_dp = lax.axis_index("dp")
        dp_bits = [lax.rem(mine_dp // (1 << b), 2) for b in range(nd)]
        dp_peers = [mine_dp + (1 - 2 * dp_bits[b]) * (1 << b) for b in range(nd)]
        for peer in dp_peers:
            pl.semaphore_signal(
                barrier, inc=1, device_id={"dp": peer}, device_id_type=pl.DeviceIdType.MESH
            )
    pl.semaphore_wait(barrier, nb + (nd if fold else 0))

    def remote(src, dst, send, recv, peer):
        return pltpu.make_async_remote_copy(
            src_ref=src, dst_ref=dst, send_sem=send, recv_sem=recv,
            device_id={"row": peer}, device_id_type=pl.DeviceIdType.MESH,
        )

    def scatter_copies(b, c):
        half = lines >> (b + 1)
        gone = pl.multiple_of(offs[b] + (1 - bits[b]) * half, half)
        d_src = acc_d if b == 0 else out_d
        return (
            remote(acc_s.at[c, pl.ds(gone, half)], in_s[b].at[c],
                   rs_send.at[0, b, c], rs_recv.at[0, b, c], peers[b]),
            remote(d_src.at[c, pl.ds(gone, half)], in_d[b].at[c],
                   rs_send.at[1, b, c], rs_recv.at[1, b, c], peers[b]),
        )

    def gather_copies(b, c):
        half = lines >> (b + 1)
        mine = pl.ds(offs[b + 1], half)
        return tuple(
            remote(ref.at[c, mine], ref.at[c, mine],
                   ag_send.at[n, b, c], ag_recv.at[n, b, c], peers[b])
            for n, ref in enumerate((probs, dsc))
        )

    def order(grp):
        inner = list(range(nd))
        if grp == 0:
            inner.reverse()
        return [("row", 0)] + [("dp", b) for b in inner] + [("row", b) for b in range(1, nb)]

    def place(grp, block):
        at = {"dp": block // group, "row": block % group}
        pos = 0
        for axis, b in order(grp):
            pos = 2 * pos + (at[axis] >> b) % 2
        return pos

    def weight_region(grp, step):
        off, size = 0, copies * group
        for axis, b in order(grp)[:step]:
            size //= 2
            off = off + (bits if axis == "row" else dp_bits)[b] * size
        return off, size

    def weight_copy(grp, step, m):
        axis, b = order(grp)[step]
        off, size = weight_region(grp, step)
        bit = (bits if axis == "row" else dp_bits)[b]
        gone = off + (1 - bit) * (size // 2)
        return pltpu.make_async_remote_copy(
            src_ref=held.at[grp, m, pl.ds(gone, size // 2)],
            dst_ref=w_in[step].at[grp, m],
            send_sem=w_send.at[grp, step, m],
            recv_sem=w_recv.at[grp, step, m],
            device_id={axis: (peers if axis == "row" else dp_peers)[b]},
            device_id_type=pl.DeviceIdType.MESH,
        )

    def weights(grp, m):
        cols = pl.ds(pl.multiple_of(m * 256, 256), 256)
        rows = width // (copies * group)
        one, two = ((x, dv), (att, g)) if grp == 0 else ((x, dq), (x, dk))
        first = dot(one[0][...], one[1][:, cols], TN)
        second = dot(two[0][...], two[1][:, cols], TN)
        for block in range(copies * group):
            at = slice(block * rows, (block + 1) * rows)
            held[grp, m, place(grp, block)] = jnp.concatenate(
                [first[at], second[at]], axis=0
            ).astype(BF)
        weight_copy(grp, 0, m).start()

    def weight_join(grp, step, m):
        weight_copy(grp, step, m).wait()
        off, size = weight_region(grp, step + 1)
        mine = pl.ds(off, size)
        total = held[grp, m, mine].astype(F32) + w_in[step][grp, m].astype(F32)
        if step + 1 < steps:
            held[grp, m, mine] = total.astype(BF)
            weight_copy(grp, step + 1, m).start()
        else:
            grads[grp, :, pl.ds(pl.multiple_of(m * 256, 256), 256)] = total[0]

    low = lax.broadcasted_iota(jnp.int32, (sites, 128), 1) < 64

    def parts(ref, c):
        cols = pl.ds(pl.multiple_of(c * 128, 128), 128)
        return [ref[r * sites : (r + 1) * sites, cols] for r in range(seqs)]

    def head_of(blocks, first):
        zero = jnp.zeros((sites, 128), BF)
        return [jnp.where(low, t, zero) if first else jnp.where(low, zero, t) for t in blocks]

    def shares(c):
        @pl.when(lax.rem(c, 2) == 0)
        def _():
            cols = pl.ds(pl.multiple_of(c * 128, 128), 256)
            q[:, cols] = dot(x[...], wq[:, cols]).astype(BF)
            k[:, cols] = dot(x[...], wk[:, cols]).astype(BF)
            v[:, cols] = dot(x[...], wv[:, cols]).astype(BF)
            do[:, cols] = dot(g[...], wo[cols, :], NT).astype(BF)

        for left, right, acc in ((q, k, acc_s), (do, v, acc_d)):
            a = jnp.concatenate(parts(left, c), axis=1)
            blocks = parts(right, c)
            for n in range(2):
                acc[c, n * sites : (n + 1) * sites, :] = dot(
                    a, jnp.concatenate(head_of(blocks, n == 0), axis=1), NT
                )
        for copy in scatter_copies(0, c):
            copy.start()

    def join(b, c):
        half = lines >> (b + 1)
        for copy in scatter_copies(b, c):
            copy.wait()
        mine = pl.ds(offs[b + 1], half)
        acc_s[c, mine, :] = acc_s[c, mine, :] + in_s[b][c]
        acc_d[c, mine, :] = acc_d[c, mine, :] + in_d[b][c].astype(F32)
        if b + 1 < nb:
            quarter = half // 2
            gone = pl.ds(
                pl.multiple_of(offs[b + 1] + (1 - bits[b + 1]) * quarter, quarter), quarter
            )
            out_d[c, gone, :] = acc_d[c, gone, :].astype(BF)
            for copy in scatter_copies(b + 1, c):
                copy.start()
        else:
            logits = acc_s[c, mine, :] * scale
            e = jnp.exp(logits - jnp.max(logits, axis=-1, keepdims=True))
            p = e / jnp.sum(e, axis=-1, keepdims=True)
            d = acc_d[c, mine, :]
            inner = jnp.sum(p * d, axis=-1, keepdims=True)
            probs[c, mine, :] = p.astype(BF)
            dsc[c, mine, :] = (p * (d - inner) * scale).astype(BF)
            for copy in gather_copies(b, c):
                copy.start()

    def spread(b, c):
        for copy in gather_copies(b, c):
            copy.wait()
        if b > 0:
            for copy in gather_copies(b - 1, c):
                copy.start()
        else:
            use(c)

    def use(c):
        cols = pl.ds(pl.multiple_of(c * 128, 128), 128)

        def stacked(ref):
            blocks = parts(ref, c)
            return jnp.concatenate(
                [jnp.concatenate(head_of(blocks, n == 0), axis=1) for n in range(2)], axis=0
            )

        def put(ref, value):
            for r in range(seqs):
                ref[r * sites : (r + 1) * sites, cols] = value[:, r * 128 : (r + 1) * 128].astype(BF)

        p = probs[c]
        d = dsc[c]
        p_wide = jnp.concatenate([p[:sites], p[sites:]], axis=1)
        d_wide = jnp.concatenate([d[:sites], d[sites:]], axis=1)
        put(att, dot(p_wide, stacked(v)))
        put(dv, dot(p, stacked(do), TN))
        put(dq, dot(d_wide, stacked(k)))
        put(dk, dot(d, stacked(q), TN))

    def rows_block(n):
        rows = pl.ds(pl.multiple_of(n * 256, 256), 256)
        dx[rows, :] = (
            dot(dq[rows, :], wq[...], NT)
            + dot(dk[rows, :], wk[...], NT)
            + dot(dv[rows, :], wv[...], NT)
        ).astype(BF)

    last = pairs + 2 * nb
    row_blocks = x.shape[0] // 256
    chunks = width // 256

    def tick(t, carry):
        if fold:
            @pl.when((t >= last) & (t < last + chunks))
            def _():
                weights(0, t - last)

        @pl.when((t >= last) & (t < last + row_blocks))
        def _():
            rows_block(t - last)

        if fold:
            for step in range(steps - 1, -1, -1):
                c = t - 2 * nb - 1 - step
                m = t - last - 1 - step

                @pl.when((c >= 0) & (c < pairs) & (lax.rem(c + pairs, 2) == 1))
                def _(step=step, c=c):
                    weight_join(1, step, c // 2)

                @pl.when((m >= 0) & (m < chunks))
                def _(step=step, m=m):
                    weight_join(0, step, m)

        for stage in range(2 * nb, -1, -1):
            c = t - stage

            @pl.when(jnp.logical_and(c >= 0, c < pairs))
            def _(stage=stage, c=c):
                if stage == 0:
                    shares(c)
                elif stage <= nb:
                    join(stage - 1, c)
                else:
                    spread(2 * nb - stage, c)
                if fold and stage == 2 * nb:
                    @pl.when(lax.rem(c, 2) == 1)
                    def _():
                        weights(1, c // 2)

        return carry

    lax.fori_loop(0, last + max(steps + chunks, row_blocks), tick, 0)
    if fold:
        return

    def weights_block(n, carry):
        base = pl.multiple_of(n * 256, 256)
        cols = pl.ds(base, 256)
        grads[:, cols] = dot(x[...], dq[:, cols], TN).astype(BF)
        grads[:, pl.ds(base + width, 256)] = dot(x[...], dk[:, cols], TN).astype(BF)
        grads[:, pl.ds(base + 2 * width, 256)] = dot(x[...], dv[:, cols], TN).astype(BF)
        grads[:, pl.ds(base + 3 * width, 256)] = dot(att[...], g[:, cols], TN).astype(BF)
        return carry

    lax.fori_loop(0, width // 256, weights_block, 0)


def body(xs, gs, wq, wk, wv, wo):
    seqs, sites, width = xs.shape[1:]
    group = lax.axis_size("row")
    nb = group.bit_length() - 1
    pairs = width // 128
    lines = 2 * sites
    n = seqs * sites
    scale = 1.0 / (math.sqrt(width // H) * math.sqrt(seqs * group))
    vmem = pl.BlockSpec(memory_space=pltpu.VMEM)
    halves = [lines >> (b + 1) for b in range(nb)]
    act = pltpu.VMEM((n, width), BF)
    scratch = [act] * 8
    scratch += [pltpu.VMEM((pairs, lines, sites), F32)] * 2
    scratch += [pltpu.VMEM((pairs, lines, sites), BF)] * 3
    scratch += [pltpu.VMEM((pairs, halves[0], sites), F32)] * 2
    scratch += [pltpu.VMEM((pairs, h, sites), F32) for h in halves[1:]]
    scratch += [pltpu.VMEM((pairs, h, sites), BF) for h in halves[1:]]
    scratch += [pltpu.SemaphoreType.DMA((2, nb, pairs))] * 4
    copies = lax.axis_size("dp")
    devices = copies * group
    own = width // devices
    fold = own % 8 == 0
    grads_shape = jax.ShapeDtypeStruct((width, 4 * width), BF)
    if fold:
        grads_shape = jax.ShapeDtypeStruct((2, 2 * own, width), F32)
        steps = devices.bit_length() - 1
        scratch += [pltpu.SemaphoreType.DMA((2, steps, width // 256))] * 2
        scratch += [
            pltpu.VMEM((2, width // 256, devices >> b, 2 * own, 256), BF) for b in range(steps + 1)
        ]
    dx, grads = pl.pallas_call(
        functools.partial(kernel, nb, group, copies, seqs, sites, scale),
        out_shape=(
            jax.ShapeDtypeStruct((n, width), BF),
            grads_shape,
        ),
        in_specs=[vmem] * 6,
        out_specs=(vmem, vmem),
        scratch_shapes=scratch,
        compiler_params=pltpu.CompilerParams(
            collective_id=0, has_side_effects=True, vmem_limit_bytes=60 * 1024 * 1024
        ),
    )(xs.reshape(n, width), gs.reshape(n, width), wq, wk, wv, wo)
    if fold:
        d_v, d_o = grads[0, :own], grads[0, own:]
        d_q, d_k = grads[1, :own], grads[1, own:]
        return dx.reshape(xs.shape), d_q, d_k, d_v, d_o
    part = lax.psum_scatter(grads, "dp", scatter_dimension=0, tiled=True)
    part = lax.psum_scatter(part, "row", scatter_dimension=0, tiled=True).astype(F32)
    return (dx.reshape(xs.shape),) + tuple(part[:, i * width : (i + 1) * width] for i in range(4))


def solution(mesh):
    return jax.shard_map(
        body,
        mesh=mesh,
        in_specs=(P("dp", "row", None, None), P("dp", "row", None, None), P(), P(), P(), P()),
        out_specs=(P("dp", "row", None, None),) + (P(("dp", "row"), None),) * 4,
        check_vma=False,
    )
```

```python
import functools
import math

import jax
import jax.numpy as jnp
from jax import lax
from jax.experimental import pallas as pl
from jax.experimental.pallas import tpu as pltpu
from jax.sharding import PartitionSpec as P

H = 12
BF = jnp.bfloat16
F32 = jnp.float32
NT = (((1,), (1,)), ((), ()))
TN = (((0,), (0,)), ((), ()))
NN = (((1,), (0,)), ((), ()))


def dot(a, b, dims=NN):
    return lax.dot_general(a, b, dims, preferred_element_type=F32)


def kernel(
    nb, group, copies, seqs, sites, scale,
    x, g, wq, wk, wv, wo,
    dx, grads,
    q, k, v, do, att, dq, dk, dv, acc_s, acc_d, probs, dsc, out_d, in0_s, in0_d, *rest,
):
    in_s = (in0_s,) + rest[: nb - 1]
    in_d = (in0_d,) + rest[nb - 1 : 2 * nb - 2]
    rs_send, rs_recv, ag_send, ag_recv = rest[2 * nb - 2 : 2 * nb + 2]
    width = x.shape[1]
    fold = grads.ndim == 3
    nd = copies.bit_length() - 1
    steps = nb + nd if fold else 0
    if fold:
        w_send, w_recv = rest[2 * nb + 2 : 2 * nb + 4]
        w_held = [rest[2 * nb + 4 + i * (steps + 1)] for i in range(3)]
        w_in = [rest[2 * nb + 5 + i * (steps + 1) : 2 * nb + 4 + (i + 1) * (steps + 1)] for i in range(3)]
    pairs = width // 128
    lines = 2 * sites
    me = lax.axis_index("row")
    bits = [lax.rem(me // (1 << b), 2) for b in range(nb)]
    peers = [me + (1 - 2 * bits[b]) * (1 << b) for b in range(nb)]
    offs = [0]
    for b in range(nb):
        offs.append(pl.multiple_of(offs[b] + bits[b] * (lines >> (b + 1)), lines >> (b + 1)))

    barrier = pltpu.get_barrier_semaphore()
    for peer in peers:
        pl.semaphore_signal(
            barrier, inc=1, device_id={"row": peer}, device_id_type=pl.DeviceIdType.MESH
        )
    if fold:
        mine_dp = lax.axis_index("dp")
        dp_bits = [lax.rem(mine_dp // (1 << b), 2) for b in range(nd)]
        dp_peers = [mine_dp + (1 - 2 * dp_bits[b]) * (1 << b) for b in range(nd)]
        for peer in dp_peers:
            pl.semaphore_signal(
                barrier, inc=1, device_id={"dp": peer}, device_id_type=pl.DeviceIdType.MESH
            )
    pl.semaphore_wait(barrier, nb + (nd if fold else 0))

    def remote(src, dst, send, recv, peer):
        return pltpu.make_async_remote_copy(
            src_ref=src, dst_ref=dst, send_sem=send, recv_sem=recv,
            device_id={"row": peer}, device_id_type=pl.DeviceIdType.MESH,
        )

    def scatter_copies(b, c):
        half = lines >> (b + 1)
        gone = pl.multiple_of(offs[b] + (1 - bits[b]) * half, half)
        d_src = acc_d if b == 0 else out_d
        return (
            remote(acc_s.at[c, pl.ds(gone, half)], in_s[b].at[c],
                   rs_send.at[0, b, c], rs_recv.at[0, b, c], peers[b]),
            remote(d_src.at[c, pl.ds(gone, half)], in_d[b].at[c],
                   rs_send.at[1, b, c], rs_recv.at[1, b, c], peers[b]),
        )

    def gather_copies(b, c):
        half = lines >> (b + 1)
        mine = pl.ds(offs[b + 1], half)
        return tuple(
            remote(ref.at[c, mine], ref.at[c, mine],
                   ag_send.at[n, b, c], ag_recv.at[n, b, c], peers[b])
            for n, ref in enumerate((probs, dsc))
        )

    def order(grp, m):
        inner = list(range(nd))
        if grp == 1 or (grp == 2 and m % 2 == 0):
            inner.reverse()
        return [("row", 0)] + [("dp", b) for b in inner] + [("row", b) for b in range(1, nb)]

    def place(grp, m, block):
        at = {"dp": block // group, "row": block % group}
        pos = 0
        for axis, b in order(grp, m):
            pos = 2 * pos + (at[axis] >> b) % 2
        return pos

    def weight_region(grp, step, m):
        off, size = 0, copies * group
        for axis, b in order(grp, m)[:step]:
            size //= 2
            off = off + (bits if axis == "row" else dp_bits)[b] * size
        return off, size

    def weight_copy(grp, step, m):
        axis, b = order(grp, m)[step]
        off, size = weight_region(grp, step, m)
        bit = (bits if axis == "row" else dp_bits)[b]
        gone = off + (1 - bit) * (size // 2)
        return pltpu.make_async_remote_copy(
            src_ref=w_held[grp].at[m, pl.ds(gone, size // 2)],
            dst_ref=w_in[grp][step].at[m],
            send_sem=w_send.at[grp, step, m],
            recv_sem=w_recv.at[grp, step, m],
            device_id={axis: (peers if axis == "row" else dp_peers)[b]},
            device_id_type=pl.DeviceIdType.MESH,
        )

    own = width // (copies * group)

    def weights(grp, m):
        if grp < 2:
            cols = pl.ds(pl.multiple_of(m * 256, 256), 256)
        if grp == 0:
            first = dot(x[...], dq[:, cols], TN)
            second = dot(x[...], dk[:, cols], TN)
        elif grp == 1:
            both = dot(x[...], dv[:, cols], TN)
            first, second = both[:, :128], both[:, 128:]
        else:
            left, right = m * 128, width // 2 + m * 128
            both = dot(
                att[...],
                jnp.concatenate([g[:, left : left + 128], g[:, right : right + 128]], axis=1),
                TN,
            )
            first, second = both[:, :128], both[:, 128:]
        for block in range(copies * group):
            at = slice(block * own, (block + 1) * own)
            w_held[grp][m, place(grp, m, block)] = jnp.concatenate(
                [first[at], second[at]], axis=0
            ).astype(BF)
        weight_copy(grp, 0, m).start()

    def weight_join(grp, step, m):
        weight_copy(grp, step, m).wait()
        off, size = weight_region(grp, step + 1, m)
        mine = pl.ds(off, size)
        total = w_held[grp][m, mine].astype(F32) + w_in[grp][step][m].astype(F32)
        if step + 1 < steps:
            w_held[grp][m, mine] = total.astype(BF)
            weight_copy(grp, step + 1, m).start()
        elif grp == 0:
            cols = pl.ds(pl.multiple_of(m * 256, 256), 256)
            grads[0, :, cols] = total[0, :own]
            grads[1, :, cols] = total[0, own:]
        elif grp == 1:
            base = pl.multiple_of(m * 256, 256)
            grads[2, :, pl.ds(base, 128)] = total[0, :own]
            grads[2, :, pl.ds(base + 128, 128)] = total[0, own:]
        else:
            left, right = m * 128, width // 2 + m * 128
            grads[3, :, left : left + 128] = total[0, :own]
            grads[3, :, right : right + 128] = total[0, own:]

    low = lax.broadcasted_iota(jnp.int32, (sites, 128), 1) < 64

    def parts(ref, c):
        cols = pl.ds(pl.multiple_of(c * 128, 128), 128)
        return [ref[r * sites : (r + 1) * sites, cols] for r in range(seqs)]

    def head_of(blocks, first):
        zero = jnp.zeros((sites, 128), BF)
        return [jnp.where(low, t, zero) if first else jnp.where(low, zero, t) for t in blocks]

    def shares(c):
        @pl.when(lax.rem(c, 2) == 0)
        def _():
            cols = pl.ds(pl.multiple_of(c * 128, 128), 256)
            q[:, cols] = dot(x[...], wq[:, cols]).astype(BF)
            k[:, cols] = dot(x[...], wk[:, cols]).astype(BF)
            v[:, cols] = dot(x[...], wv[:, cols]).astype(BF)
            do[:, cols] = dot(g[...], wo[cols, :], NT).astype(BF)

        for left, right, acc in ((q, k, acc_s), (do, v, acc_d)):
            a = jnp.concatenate(parts(left, c), axis=1)
            blocks = parts(right, c)
            for n in range(2):
                acc[c, n * sites : (n + 1) * sites, :] = dot(
                    a, jnp.concatenate(head_of(blocks, n == 0), axis=1), NT
                )
        for copy in scatter_copies(0, c):
            copy.start()

    def join(b, c):
        half = lines >> (b + 1)
        for copy in scatter_copies(b, c):
            copy.wait()
        mine = pl.ds(offs[b + 1], half)
        acc_s[c, mine, :] = acc_s[c, mine, :] + in_s[b][c]
        acc_d[c, mine, :] = acc_d[c, mine, :] + in_d[b][c].astype(F32)
        if b + 1 < nb:
            quarter = half // 2
            gone = pl.ds(
                pl.multiple_of(offs[b + 1] + (1 - bits[b + 1]) * quarter, quarter), quarter
            )
            out_d[c, gone, :] = acc_d[c, gone, :].astype(BF)
            for copy in scatter_copies(b + 1, c):
                copy.start()
        else:
            logits = acc_s[c, mine, :] * scale
            e = jnp.exp(logits - jnp.max(logits, axis=-1, keepdims=True))
            p = e / jnp.sum(e, axis=-1, keepdims=True)
            d = acc_d[c, mine, :]
            inner = jnp.sum(p * d, axis=-1, keepdims=True)
            probs[c, mine, :] = p.astype(BF)
            dsc[c, mine, :] = (p * (d - inner) * scale).astype(BF)
            for copy in gather_copies(b, c):
                copy.start()

    def spread(b, c):
        for copy in gather_copies(b, c):
            copy.wait()
        if b > 0:
            for copy in gather_copies(b - 1, c):
                copy.start()
        else:
            use(c)

    def use(c):
        cols = pl.ds(pl.multiple_of(c * 128, 128), 128)

        def stacked(ref):
            blocks = parts(ref, c)
            return jnp.concatenate(
                [jnp.concatenate(head_of(blocks, n == 0), axis=1) for n in range(2)], axis=0
            )

        def put(ref, value):
            for r in range(seqs):
                ref[r * sites : (r + 1) * sites, cols] = value[:, r * 128 : (r + 1) * 128].astype(BF)

        p = probs[c]
        d = dsc[c]
        p_wide = jnp.concatenate([p[:sites], p[sites:]], axis=1)
        d_wide = jnp.concatenate([d[:sites], d[sites:]], axis=1)
        put(att, dot(p_wide, stacked(v)))
        put(dv, dot(p, stacked(do), TN))
        put(dq, dot(d_wide, stacked(k)))
        put(dk, dot(d, stacked(q), TN))

    def rows_block(n):
        rows = pl.ds(pl.multiple_of(n * 256, 256), 256)
        dx[rows, :] = (
            dot(dq[rows, :], wq[...], NT)
            + dot(dk[rows, :], wk[...], NT)
            + dot(dv[rows, :], wv[...], NT)
        ).astype(BF)

    last = pairs + 2 * nb
    row_blocks = x.shape[0] // 256
    chunks = width // 256

    def tick(t, carry):
        if fold:
            @pl.when(t == last)
            def _():
                for m in range(chunks):
                    weights(2, m)

        @pl.when((t >= last) & (t < last + row_blocks))
        def _():
            rows_block(t - last)

        if fold:
            for step in range(steps - 1, -1, -1):
                c = t - 2 * nb - 1 - step

                @pl.when((c >= 0) & (c < pairs) & (lax.rem(c + pairs, 2) == 1))
                def _(step=step, c=c):
                    weight_join(0, step, c // 2)
                    weight_join(1, step, c // 2)

                @pl.when(t == last + 1 + step)
                def _(step=step):
                    for m in range(chunks):
                        weight_join(2, step, m)

        for stage in range(2 * nb, -1, -1):
            c = t - stage

            @pl.when(jnp.logical_and(c >= 0, c < pairs))
            def _(stage=stage, c=c):
                if stage == 0:
                    shares(c)
                elif stage <= nb:
                    join(stage - 1, c)
                else:
                    spread(2 * nb - stage, c)
                if fold and stage == 2 * nb:
                    @pl.when(lax.rem(c, 2) == 1)
                    def _():
                        weights(0, c // 2)
                        weights(1, c // 2)

        return carry

    lax.fori_loop(0, last + max(steps + 1, row_blocks), tick, 0)
    if fold:
        return

    def weights_block(n, carry):
        base = pl.multiple_of(n * 256, 256)
        cols = pl.ds(base, 256)
        grads[:, cols] = dot(x[...], dq[:, cols], TN).astype(BF)
        grads[:, pl.ds(base + width, 256)] = dot(x[...], dk[:, cols], TN).astype(BF)
        grads[:, pl.ds(base + 2 * width, 256)] = dot(x[...], dv[:, cols], TN).astype(BF)
        grads[:, pl.ds(base + 3 * width, 256)] = dot(att[...], g[:, cols], TN).astype(BF)
        return carry

    lax.fori_loop(0, width // 256, weights_block, 0)


def body(xs, gs, wq, wk, wv, wo):
    seqs, sites, width = xs.shape[1:]
    group = lax.axis_size("row")
    nb = group.bit_length() - 1
    pairs = width // 128
    lines = 2 * sites
    n = seqs * sites
    scale = 1.0 / (math.sqrt(width // H) * math.sqrt(seqs * group))
    vmem = pl.BlockSpec(memory_space=pltpu.VMEM)
    halves = [lines >> (b + 1) for b in range(nb)]
    act = pltpu.VMEM((n, width), BF)
    scratch = [act] * 8
    scratch += [pltpu.VMEM((pairs, lines, sites), F32)] * 2
    scratch += [pltpu.VMEM((pairs, lines, sites), BF)] * 3
    scratch += [pltpu.VMEM((pairs, halves[0], sites), F32)] * 2
    scratch += [pltpu.VMEM((pairs, h, sites), F32) for h in halves[1:]]
    scratch += [pltpu.VMEM((pairs, h, sites), BF) for h in halves[1:]]
    scratch += [pltpu.SemaphoreType.DMA((2, nb, pairs))] * 4
    copies = lax.axis_size("dp")
    devices = copies * group
    own = width // devices
    fold = own % 8 == 0
    grads_shape = jax.ShapeDtypeStruct((width, 4 * width), BF)
    if fold:
        grads_shape = jax.ShapeDtypeStruct((4, own, width), F32)
        steps = devices.bit_length() - 1
        scratch += [pltpu.SemaphoreType.DMA((3, steps, width // 256))] * 2
        scratch += [
            pltpu.VMEM((width // 256, devices >> b, 2 * own, lanes), BF)
            for lanes in (256, 128, 128)
            for b in range(steps + 1)
        ]
    dx, grads = pl.pallas_call(
        functools.partial(kernel, nb, group, copies, seqs, sites, scale),
        out_shape=(
            jax.ShapeDtypeStruct((n, width), BF),
            grads_shape,
        ),
        in_specs=[vmem] * 6,
        out_specs=(vmem, vmem),
        scratch_shapes=scratch,
        compiler_params=pltpu.CompilerParams(
            collective_id=0, has_side_effects=True, vmem_limit_bytes=60 * 1024 * 1024
        ),
    )(xs.reshape(n, width), gs.reshape(n, width), wq, wk, wv, wo)
    if fold:
        return (dx.reshape(xs.shape),) + tuple(grads[i] for i in range(4))
    part = lax.psum_scatter(grads, "dp", scatter_dimension=0, tiled=True)
    part = lax.psum_scatter(part, "row", scatter_dimension=0, tiled=True).astype(F32)
    return (dx.reshape(xs.shape),) + tuple(part[:, i * width : (i + 1) * width] for i in range(4))


def solution(mesh):
    return jax.shard_map(
        body,
        mesh=mesh,
        in_specs=(P("dp", "row", None, None), P("dp", "row", None, None), P(), P(), P(), P()),
        out_specs=(P("dp", "row", None, None),) + (P(("dp", "row"), None),) * 4,
        check_vma=False,
    )
```

```python
import functools
import math

import jax
import jax.numpy as jnp
from jax import lax
from jax.experimental import pallas as pl
from jax.experimental.pallas import tpu as pltpu
from jax.sharding import PartitionSpec as P

H = 12
BF = jnp.bfloat16
F32 = jnp.float32
NT = (((1,), (1,)), ((), ()))
TN = (((0,), (0,)), ((), ()))
NN = (((1,), (0,)), ((), ()))


def dot(a, b, dims=NN):
    return lax.dot_general(a, b, dims, preferred_element_type=F32)


def kernel(
    nb, group, copies, seqs, sites, scale,
    x, g, wq, wk, wv, wo,
    dx, grads,
    q, k, v, do, att, dq, dk, dv, acc_s, acc_d, probs, dsc, out_d, in0_s, in0_d, *rest,
):
    in_s = (in0_s,) + rest[: nb - 1]
    in_d = (in0_d,) + rest[nb - 1 : 2 * nb - 2]
    rs_send, rs_recv, ag_send, ag_recv = rest[2 * nb - 2 : 2 * nb + 2]
    width = x.shape[1]
    fold = grads.ndim == 3
    nd = copies.bit_length() - 1
    steps = nb + nd if fold else 0
    if fold:
        w_send, w_recv = rest[2 * nb + 2 : 2 * nb + 4]
        w_held = [rest[2 * nb + 4 + i * (steps + 1)] for i in range(3)]
        w_in = [rest[2 * nb + 5 + i * (steps + 1) : 2 * nb + 4 + (i + 1) * (steps + 1)] for i in range(3)]
    pairs = width // 128
    lines = 2 * sites
    me = lax.axis_index("row")
    bits = [lax.rem(me // (1 << b), 2) for b in range(nb)]
    peers = [me + (1 - 2 * bits[b]) * (1 << b) for b in range(nb)]
    offs = [0]
    for b in range(nb):
        offs.append(pl.multiple_of(offs[b] + bits[b] * (lines >> (b + 1)), lines >> (b + 1)))

    barrier = pltpu.get_barrier_semaphore()
    for peer in peers:
        pl.semaphore_signal(
            barrier, inc=1, device_id={"row": peer}, device_id_type=pl.DeviceIdType.MESH
        )
    if fold:
        mine_dp = lax.axis_index("dp")
        dp_bits = [lax.rem(mine_dp // (1 << b), 2) for b in range(nd)]
        dp_peers = [mine_dp + (1 - 2 * dp_bits[b]) * (1 << b) for b in range(nd)]
        for peer in dp_peers:
            pl.semaphore_signal(
                barrier, inc=1, device_id={"dp": peer}, device_id_type=pl.DeviceIdType.MESH
            )
    pl.semaphore_wait(barrier, nb + (nd if fold else 0))

    def remote(src, dst, send, recv, peer):
        return pltpu.make_async_remote_copy(
            src_ref=src, dst_ref=dst, send_sem=send, recv_sem=recv,
            device_id={"row": peer}, device_id_type=pl.DeviceIdType.MESH,
        )

    def scatter_copies(b, c):
        half = lines >> (b + 1)
        gone = pl.multiple_of(offs[b] + (1 - bits[b]) * half, half)
        d_src = acc_d if b == 0 else out_d
        return (
            remote(acc_s.at[c, pl.ds(gone, half)], in_s[b].at[c],
                   rs_send.at[0, b, c], rs_recv.at[0, b, c], peers[b]),
            remote(d_src.at[c, pl.ds(gone, half)], in_d[b].at[c],
                   rs_send.at[1, b, c], rs_recv.at[1, b, c], peers[b]),
        )

    def gather_copies(b, c):
        half = lines >> (b + 1)
        mine = pl.ds(offs[b + 1], half)
        return tuple(
            remote(ref.at[c, mine], ref.at[c, mine],
                   ag_send.at[n, b, c], ag_recv.at[n, b, c], peers[b])
            for n, ref in enumerate((probs, dsc))
        )

    def order(grp, m):
        inner = list(range(nd))
        if grp == 1 or (grp == 2 and m % 2 == 0):
            inner.reverse()
        return [("row", 0)] + [("dp", b) for b in inner] + [("row", b) for b in range(1, nb)]

    def place(grp, m, block):
        at = {"dp": block // group, "row": block % group}
        pos = 0
        for axis, b in order(grp, m):
            pos = 2 * pos + (at[axis] >> b) % 2
        return pos

    def weight_region(grp, step, m):
        off, size = 0, copies * group
        for axis, b in order(grp, m)[:step]:
            size //= 2
            off = off + (bits if axis == "row" else dp_bits)[b] * size
        return off, size

    def weight_copy(grp, step, m):
        axis, b = order(grp, m)[step]
        off, size = weight_region(grp, step, m)
        bit = (bits if axis == "row" else dp_bits)[b]
        gone = off + (1 - bit) * (size // 2)
        return pltpu.make_async_remote_copy(
            src_ref=w_held[grp].at[m, pl.ds(gone, size // 2)],
            dst_ref=w_in[grp][step].at[m],
            send_sem=w_send.at[grp, step, m],
            recv_sem=w_recv.at[grp, step, m],
            device_id={axis: (peers if axis == "row" else dp_peers)[b]},
            device_id_type=pl.DeviceIdType.MESH,
        )

    own = width // (copies * group)

    def weights(grp, m):
        if grp < 2:
            cols = pl.ds(pl.multiple_of(m * 256, 256), 256)
        if grp == 0:
            first = dot(x[...], dq[:, cols], TN)
            second = dot(x[...], dk[:, cols], TN)
        elif grp == 1:
            both = dot(x[...], dv[:, cols], TN)
            first, second = both[:, :128], both[:, 128:]
        else:
            left, right = m * 128, width // 2 + m * 128
            both = dot(
                att[...],
                jnp.concatenate([g[:, left : left + 128], g[:, right : right + 128]], axis=1),
                TN,
            )
            first, second = both[:, :128], both[:, 128:]
        for block in range(copies * group):
            at = slice(block * own, (block + 1) * own)
            w_held[grp][m, place(grp, m, block)] = jnp.concatenate(
                [first[at], second[at]], axis=0
            ).astype(BF)
        weight_copy(grp, 0, m).start()

    def weight_join(grp, step, m):
        weight_copy(grp, step, m).wait()
        off, size = weight_region(grp, step + 1, m)
        mine = pl.ds(off, size)
        total = w_held[grp][m, mine].astype(F32) + w_in[grp][step][m].astype(F32)
        if step + 1 < steps:
            w_held[grp][m, mine] = total.astype(BF)
            weight_copy(grp, step + 1, m).start()
        elif grp == 0:
            cols = pl.ds(pl.multiple_of(m * 256, 256), 256)
            grads[0, :, cols] = total[0, :own]
            grads[1, :, cols] = total[0, own:]
        elif grp == 1:
            base = pl.multiple_of(m * 256, 256)
            grads[2, :, pl.ds(base, 128)] = total[0, :own]
            grads[2, :, pl.ds(base + 128, 128)] = total[0, own:]
        else:
            left, right = m * 128, width // 2 + m * 128
            grads[3, :, left : left + 128] = total[0, :own]
            grads[3, :, right : right + 128] = total[0, own:]

    low = lax.broadcasted_iota(jnp.int32, (sites, 128), 1) < 64

    def parts(ref, c):
        cols = pl.ds(pl.multiple_of(c * 128, 128), 128)
        return [ref[r * sites : (r + 1) * sites, cols] for r in range(seqs)]

    def head_of(blocks, first):
        zero = jnp.zeros((sites, 128), BF)
        return [jnp.where(low, t, zero) if first else jnp.where(low, zero, t) for t in blocks]

    def shares(c):
        @pl.when(lax.rem(c, 2) == 0)
        def _():
            cols = pl.ds(pl.multiple_of(c * 128, 128), 256)
            q[:, cols] = dot(x[...], wq[:, cols]).astype(BF)
            k[:, cols] = dot(x[...], wk[:, cols]).astype(BF)
            v[:, cols] = dot(x[...], wv[:, cols]).astype(BF)
            do[:, cols] = dot(g[...], wo[cols, :], NT).astype(BF)

        for left, right, acc in ((q, k, acc_s), (do, v, acc_d)):
            a = jnp.concatenate(parts(left, c), axis=1)
            blocks = parts(right, c)
            for n in range(2):
                acc[c, n * sites : (n + 1) * sites, :] = dot(
                    a, jnp.concatenate(head_of(blocks, n == 0), axis=1), NT
                )
        for copy in scatter_copies(0, c):
            copy.start()

    def join(b, c):
        half = lines >> (b + 1)
        for copy in scatter_copies(b, c):
            copy.wait()
        mine = pl.ds(offs[b + 1], half)
        acc_s[c, mine, :] = acc_s[c, mine, :] + in_s[b][c]
        acc_d[c, mine, :] = acc_d[c, mine, :] + in_d[b][c].astype(F32)
        if b + 1 < nb:
            quarter = half // 2
            gone = pl.ds(
                pl.multiple_of(offs[b + 1] + (1 - bits[b + 1]) * quarter, quarter), quarter
            )
            out_d[c, gone, :] = acc_d[c, gone, :].astype(BF)
            for copy in scatter_copies(b + 1, c):
                copy.start()
        else:
            logits = acc_s[c, mine, :] * scale
            e = jnp.exp(logits - jnp.max(logits, axis=-1, keepdims=True))
            p = e / jnp.sum(e, axis=-1, keepdims=True)
            d = acc_d[c, mine, :]
            inner = jnp.sum(p * d, axis=-1, keepdims=True)
            probs[c, mine, :] = p.astype(BF)
            dsc[c, mine, :] = (p * (d - inner) * scale).astype(BF)
            for copy in gather_copies(b, c):
                copy.start()

    def spread(b, c):
        for copy in gather_copies(b, c):
            copy.wait()
        if b > 0:
            for copy in gather_copies(b - 1, c):
                copy.start()
        else:
            use(c)

    def use(c):
        cols = pl.ds(pl.multiple_of(c * 128, 128), 128)

        def stacked(ref):
            blocks = parts(ref, c)
            return jnp.concatenate(
                [jnp.concatenate(head_of(blocks, n == 0), axis=1) for n in range(2)], axis=0
            )

        def put(ref, value):
            for r in range(seqs):
                ref[r * sites : (r + 1) * sites, cols] = value[:, r * 128 : (r + 1) * 128].astype(BF)

        p = probs[c]
        d = dsc[c]
        p_wide = jnp.concatenate([p[:sites], p[sites:]], axis=1)
        d_wide = jnp.concatenate([d[:sites], d[sites:]], axis=1)
        put(att, dot(p_wide, stacked(v)))
        put(dv, dot(p, stacked(do), TN))
        put(dq, dot(d_wide, stacked(k)))
        put(dk, dot(d, stacked(q), TN))

    def rows_block(n):
        rows = pl.ds(pl.multiple_of(n * 256, 256), 256)
        dx[rows, :] = (
            dot(dq[rows, :], wq[...], NT)
            + dot(dk[rows, :], wk[...], NT)
            + dot(dv[rows, :], wv[...], NT)
        ).astype(BF)

    last = pairs + 2 * nb
    row_blocks = x.shape[0] // 256
    chunks = width // 256

    def tick(t, carry):
        def run(stages):
            for stage in stages:
                c = t - stage

                @pl.when(jnp.logical_and(c >= 0, c < pairs))
                def _(stage=stage, c=c):
                    if stage == 0:
                        shares(c)
                    elif stage <= nb:
                        join(stage - 1, c)
                    else:
                        spread(2 * nb - stage, c)
                    if fold and stage == 2 * nb:
                        @pl.when(lax.rem(c, 2) == 1)
                        def _():
                            weights(0, c // 2)
                            weights(1, c // 2)

        run(range(2 * nb - 1, -1, -1))
        if fold:
            @pl.when(t == last)
            def _():
                for m in range(chunks):
                    weights(2, m)

        @pl.when((t >= last) & (t < last + row_blocks))
        def _():
            rows_block(t - last)

        if fold:
            for step in range(steps - 1, -1, -1):
                c = t - 2 * nb - 1 - step

                @pl.when((c >= 0) & (c < pairs) & (lax.rem(c + pairs, 2) == 1))
                def _(step=step, c=c):
                    weight_join(0, step, c // 2)
                    weight_join(1, step, c // 2)

                @pl.when(t == last + 1 + step)
                def _(step=step):
                    for m in range(chunks):
                        weight_join(2, step, m)

        run((2 * nb,))
        return carry

    lax.fori_loop(0, last + max(steps + 1, row_blocks), tick, 0)
    if fold:
        return

    def weights_block(n, carry):
        base = pl.multiple_of(n * 256, 256)
        cols = pl.ds(base, 256)
        grads[:, cols] = dot(x[...], dq[:, cols], TN).astype(BF)
        grads[:, pl.ds(base + width, 256)] = dot(x[...], dk[:, cols], TN).astype(BF)
        grads[:, pl.ds(base + 2 * width, 256)] = dot(x[...], dv[:, cols], TN).astype(BF)
        grads[:, pl.ds(base + 3 * width, 256)] = dot(att[...], g[:, cols], TN).astype(BF)
        return carry

    lax.fori_loop(0, width // 256, weights_block, 0)


def body(xs, gs, wq, wk, wv, wo):
    seqs, sites, width = xs.shape[1:]
    group = lax.axis_size("row")
    nb = group.bit_length() - 1
    pairs = width // 128
    lines = 2 * sites
    n = seqs * sites
    scale = 1.0 / (math.sqrt(width // H) * math.sqrt(seqs * group))
    vmem = pl.BlockSpec(memory_space=pltpu.VMEM)
    halves = [lines >> (b + 1) for b in range(nb)]
    act = pltpu.VMEM((n, width), BF)
    scratch = [act] * 8
    scratch += [pltpu.VMEM((pairs, lines, sites), F32)] * 2
    scratch += [pltpu.VMEM((pairs, lines, sites), BF)] * 3
    scratch += [pltpu.VMEM((pairs, halves[0], sites), F32)] * 2
    scratch += [pltpu.VMEM((pairs, h, sites), F32) for h in halves[1:]]
    scratch += [pltpu.VMEM((pairs, h, sites), BF) for h in halves[1:]]
    scratch += [pltpu.SemaphoreType.DMA((2, nb, pairs))] * 4
    copies = lax.axis_size("dp")
    devices = copies * group
    own = width // devices
    fold = own % 8 == 0
    grads_shape = jax.ShapeDtypeStruct((width, 4 * width), BF)
    if fold:
        grads_shape = jax.ShapeDtypeStruct((4, own, width), F32)
        steps = devices.bit_length() - 1
        scratch += [pltpu.SemaphoreType.DMA((3, steps, width // 256))] * 2
        scratch += [
            pltpu.VMEM((width // 256, devices >> b, 2 * own, lanes), BF)
            for lanes in (256, 128, 128)
            for b in range(steps + 1)
        ]
    dx, grads = pl.pallas_call(
        functools.partial(kernel, nb, group, copies, seqs, sites, scale),
        out_shape=(
            jax.ShapeDtypeStruct((n, width), BF),
            grads_shape,
        ),
        in_specs=[vmem] * 6,
        out_specs=(vmem, vmem),
        scratch_shapes=scratch,
        compiler_params=pltpu.CompilerParams(
            collective_id=0, has_side_effects=True, vmem_limit_bytes=60 * 1024 * 1024
        ),
    )(xs.reshape(n, width), gs.reshape(n, width), wq, wk, wv, wo)
    if fold:
        return (dx.reshape(xs.shape),) + tuple(grads[i] for i in range(4))
    part = lax.psum_scatter(grads, "dp", scatter_dimension=0, tiled=True)
    part = lax.psum_scatter(part, "row", scatter_dimension=0, tiled=True).astype(F32)
    return (dx.reshape(xs.shape),) + tuple(part[:, i * width : (i + 1) * width] for i in range(4))


def solution(mesh):
    return jax.shard_map(
        body,
        mesh=mesh,
        in_specs=(P("dp", "row", None, None), P("dp", "row", None, None), P(), P(), P(), P()),
        out_specs=(P("dp", "row", None, None),) + (P(("dp", "row"), None),) * 4,
        check_vma=False,
    )
```
